512 devices in a mesh: blk: 128 (over y, z, x_hi), head: 4 (over x_lo, core).
Axes of the slice: x: 4 (x_hi: 2, x_lo: 2; x = x_hi * 2 + x_lo), y: 4, z: 16, core: 2. Of those that a mesh axis runs over, the one named last changes fastest.
Arguments:
- query: bfloat16 [4, 512, 32, 512], P('head', 'blk'), may hold values from -8 to 8
- keyset: bfloat16 [4, 512, 32, 512], P('head', 'blk'), may hold values from -8 to 8
- values: bfloat16 [4, 512, 32, 512], P('head', 'blk'), may hold values from -6 to 6
- cotangent: bfloat16 [4, 512, 32, 512], P('head', 'blk'), may hold values from -24 to 24
- pair_norm: bfloat16 [128, 512, 512], P('head', 'blk'), may hold values from -6 to 6
- bias_weight: bfloat16 [128, 4], P('head'), may hold values from -0.5 to 0.5
Outputs:
- grad_query: bfloat16 [4, 512, 32, 512], P('head', 'blk')
- grad_key: bfloat16 [4, 512, 32, 512], P('head', 'blk')
- grad_value: bfloat16 [4, 512, 32, 512], P('head', 'blk')
- grad_pair: float32 [128, 512, 512], P('head', 'blk')
The draws below stay inside these ranges and needn't reach their ends.
All inputs are finite; a program needn't handle non-finite values.
Results may differ from the reference program's by a relative error of at most 0.012.
Values may be sent and summed in bfloat16 or wider, within the bound.
No kernel may reach another device: no remote copies, remote signals or barrier semaphores. Data moves between devices by JAX's collectives and lax.ppermute only.
A program may use at most 64 MiB of HBM per device.

```python
import jax
import jax.numpy as jnp
from jax import lax

C = 128
H = 4
DH = 32
L = 512


def draw_query(key, part):
    key = jax.random.fold_in(key, 11)
    drawn = jnp.clip(jax.random.normal(key, (H, L, DH, L)), -4.0, 4.0)
    return drawn.astype(jnp.bfloat16)


def draw_keyset(key, part):
    key = jax.random.fold_in(key, 23)
    drawn = jnp.clip(jax.random.normal(key, (H, L, DH, L)), -4.0, 4.0)
    return drawn.astype(jnp.bfloat16)


def raised(array, own_key, source, target, blocks, factor):
    owner, partner = [(jnp.arange(array.shape[axis_at]) // (array.shape[axis_at] // blocks)).reshape([-1 if axis == axis_at else 1 for axis in range(array.ndim)]) for axis_at in (source, target)]
    chosen = jax.random.permutation(own_key, blocks)[partner]
    strong = (owner == chosen) | (owner == (partner + blocks // 2) % blocks)
    return jnp.where(strong, factor * array, array)


def levels(key, shape, shards, low, largest):
    factor_of, own = 1.0, jax.random.fold_in(key, 6)
    for dim, blocks in shards:
        heights = jnp.exp(jax.random.uniform(jax.random.fold_in(own, dim), (blocks,), jnp.float32, low / len(shards), largest / len(shards)))
        factor_of = factor_of * jnp.repeat(heights, shape[dim] // blocks).reshape([-1 if axis == dim else 1 for axis in range(len(shape))])
    return factor_of


def gaussian(rng, shape, scale, reach, cuts=(), dtype=jnp.bfloat16):
    factor_of = levels(rng, shape, cuts, -0.22, 0.18) if cuts else 1.0
    drawn = jax.random.normal(rng, shape, jnp.float32) * scale * factor_of
    return jnp.minimum(jnp.maximum(drawn, -reach), reach).astype(dtype)


def heavy_noise(rng, extent, width, bound, cuts, heavy, held_as=jnp.bfloat16):
    drawn = width * jax.random.normal(rng, extent, jnp.float32)
    if cuts:
        drawn = drawn * levels(rng, extent, cuts, -0.22, 0.18)
    return jnp.clip(raised(drawn, jax.random.fold_in(rng, 3), *heavy), -bound, bound).astype(held_as)


def setup_inputs(seed: int = 0) -> dict:
    arg_keys = jax.random.split(jax.random.key(seed), 7)
    query = draw_query(jax.random.fold_in(arg_keys[6], 71), 0)
    keyset = draw_keyset(jax.random.fold_in(arg_keys[6], 71), 0)
    values = gaussian(arg_keys[2], (H, L, DH, L), 1.0, 6.0, ((0, 4), (1, 128)))
    cotangent = heavy_noise(arg_keys[3], (H, L, DH, L), 1.0, 24.0, ((0, 4), (1, 128)), (1, 3, 128, 5.5))
    pair_norm = gaussian(arg_keys[4], (C, L, L), 1.0, 6.0, ((0, 4), (1, 128)))
    bias_weight = gaussian(arg_keys[5], (C, H), C ** -0.5, 0.5, ((0, 4),))
    return dict(query=query, keyset=keyset, values=values, cotangent=cotangent, pair_norm=pair_norm, bias_weight=bias_weight)


def row_grads(query_row, key_row, value_row, cotan_row, bias):
    scale_factor = DH ** -0.5
    query_wide = query_row.astype(jnp.float32)
    key_wide = key_row.astype(jnp.float32)
    value_wide = value_row.astype(jnp.float32)
    cotan_wide = cotan_row.astype(jnp.float32)
    scores = jnp.einsum("hdj,hdk->hjk", query_wide, key_wide) * scale_factor + bias.astype(jnp.float32)
    highest = jnp.max(scores, axis=-1, keepdims=True)
    weights = jnp.exp(scores - highest)
    probs = weights / jnp.sum(weights, axis=-1, keepdims=True)
    probs_low = lax.optimization_barrier(probs.astype(jnp.bfloat16)).astype(jnp.float32)
    output = jnp.einsum("hjk,hdk->hdj", probs_low, value_wide)
    delta = jnp.sum(cotan_wide * output, axis=1)
    dprobs = jnp.einsum("hdj,hdk->hjk", cotan_wide, value_wide)
    dscores = probs * (dprobs - delta[:, :, None])
    dscores_low = lax.optimization_barrier(dscores.astype(jnp.bfloat16)).astype(jnp.float32)
    grad_q = jnp.einsum("hjk,hdk->hdj", dscores_low, key_wide) * scale_factor
    grad_k = jnp.einsum("hjk,hdj->hdk", dscores_low, query_wide) * scale_factor
    grad_v = jnp.einsum("hjk,hdj->hdk", probs_low, cotan_wide)
    return grad_q.astype(jnp.bfloat16), grad_k.astype(jnp.bfloat16), grad_v.astype(jnp.bfloat16), dscores


def reference(query, keyset, values, cotangent, pair_norm, bias_weight):
    weight_wide = bias_weight.astype(jnp.float32)
    bias = jnp.einsum("ch,cjk->hjk", weight_wide, pair_norm.astype(jnp.float32), precision=lax.Precision.HIGHEST).astype(jnp.bfloat16)

    def advance(total, inputs):
        query_row, key_row, value_row, cotan_row = inputs
        grad_q, grad_k, grad_v, dscores = row_grads(query_row, key_row, value_row, cotan_row, bias)
        return total + dscores, (grad_q, grad_k, grad_v)

    stacked = (jnp.moveaxis(query, 1, 0), jnp.moveaxis(keyset, 1, 0), jnp.moveaxis(values, 1, 0), jnp.moveaxis(cotangent, 1, 0))
    grad_bias, (grad_q, grad_k, grad_v) = lax.scan(advance, jnp.zeros((H, L, L), jnp.float32), stacked)
    grad_pair = jnp.einsum("ch,hjk->cjk", weight_wide, grad_bias, precision=lax.Precision.HIGHEST)
    return jnp.moveaxis(grad_q, 0, 1), jnp.moveaxis(grad_k, 0, 1), jnp.moveaxis(grad_v, 0, 1), grad_pair
```

```python
import jax
import jax.numpy as jnp
from jax import lax
from jax.sharding import Mesh
from jax.sharding import PartitionSpec as P

DH = 32
BLK = ("y", "z", "xh")
HEAD = ("xl", "core")
RING = ("xh", "xl", "core")


def attend_grads(query_rows, key_rows, value_rows, cotan_rows, bias_rows):
    scale_factor = DH ** (-0.5)
    scores = (
        jnp.einsum("rdj,rdk->rjk", query_rows, key_rows, preferred_element_type=jnp.float32)
        * scale_factor
    )
    scores = scores + bias_rows.astype(jnp.float32)[None]
    highest = jnp.max(scores, axis=-1, keepdims=True)
    weights = jnp.exp(scores - highest)
    probs = weights / jnp.sum(weights, axis=-1, keepdims=True)
    probs_low = probs.astype(jnp.bfloat16)
    output = jnp.einsum("rjk,rdk->rdj", probs_low, value_rows, preferred_element_type=jnp.float32)
    delta = jnp.sum(cotan_rows.astype(jnp.float32) * output, axis=1)
    dprobs = jnp.einsum("rdj,rdk->rjk", cotan_rows, value_rows, preferred_element_type=jnp.float32)
    dscores = probs * (dprobs - delta[..., None])
    dscores_low = dscores.astype(jnp.bfloat16)
    grad_q = (
        jnp.einsum("rjk,rdk->rdj", dscores_low, key_rows, preferred_element_type=jnp.float32)
        * scale_factor
    )
    grad_k = (
        jnp.einsum("rjk,rdj->rdk", dscores_low, query_rows, preferred_element_type=jnp.float32)
        * scale_factor
    )
    grad_v = jnp.einsum("rjk,rdj->rdk", probs_low, cotan_rows, preferred_element_type=jnp.float32)
    return (
        grad_q.astype(jnp.bfloat16),
        grad_k.astype(jnp.bfloat16),
        grad_v.astype(jnp.bfloat16),
        jnp.sum(dscores, axis=0),
    )


def exchange(blocks, axes):
    return lax.all_to_all(blocks, axes, 0, 0, tiled=True)


def shards(query, keyset, values, cotangent, pair_norm, bias_weight):
    ny, nz, nx = lax.axis_size("y"), lax.axis_size("z"), lax.axis_size("xh")
    nh = lax.axis_size(HEAD)
    rows, width = pair_norm.shape[1:]
    partial = jnp.einsum("ch,cjk->hjk", bias_weight, pair_norm, preferred_element_type=jnp.float32)
    sent = jnp.broadcast_to(partial[None], (nx, nh, rows, width)).reshape(nx * nh, rows, width)
    parts = exchange(sent, RING).reshape(nx, nh, rows, width)
    own = jnp.sum(parts, axis=1).astype(jnp.bfloat16).reshape(nx * rows, width)
    plane = exchange(jnp.broadcast_to(own[None], (nz,) + own.shape), "z")
    plane = plane.reshape(nz * nx * rows, width)
    full = exchange(jnp.broadcast_to(plane[None], (ny,) + plane.shape), "y")
    full = full.reshape(ny * nz * nx * rows, width)

    grad_q, grad_k, grad_v, grad_bias = attend_grads(
        query[0], keyset[0], values[0], cotangent[0], full
    )

    low = grad_bias.astype(jnp.bfloat16).reshape(ny, nz * nx * rows, width)
    plane = jnp.sum(exchange(low, "y").astype(jnp.float32), axis=0).astype(jnp.bfloat16)
    plane = exchange(plane.reshape(nz, nx * rows, width), "z")
    own = jnp.sum(plane.astype(jnp.float32), axis=0).reshape(nx, 1, rows, width)
    sent = jnp.broadcast_to(own, (nx, nh, rows, width)).reshape(nx * nh, rows, width)
    every_head = jnp.sum(exchange(sent, RING).reshape(nx, nh, rows, width), axis=0)
    grad_pair = jnp.einsum(
        "ch,hjk->cjk", bias_weight.astype(jnp.float32), every_head, precision=lax.Precision.HIGHEST
    )
    return grad_q[None], grad_k[None], grad_v[None], grad_pair


def solution(mesh):
    fine = Mesh(mesh.devices.reshape(4, 16, 2, 2, 2), BLK + HEAD)
    four = P(HEAD, BLK, None, None)
    three = P(HEAD, BLK, None)
    return jax.shard_map(
        shards,
        mesh=fine,
        in_specs=(four, four, four, four, three, P(HEAD, None)),
        out_specs=(four, four, four, three),
        check_vma=False,
    )
```

```python
import jax
import jax.numpy as jnp
from jax import lax
from jax.experimental import pallas as pl
from jax.experimental.pallas import tpu as pltpu
from jax.sharding import Mesh
from jax.sharding import PartitionSpec as P

DH = 32
BLK = ("y", "z", "xh")
HEAD = ("xl", "core")
RING = ("xh", "xl", "core")
TILE = 128
LIMIT = 48 * 1024 * 1024


def scores_kernel(query, keyset, values, cotangent, bias, total, probs_low, dscores_low):
    wide = bias[...].astype(jnp.float32)
    summed = None
    for row in range(query.shape[0]):
        scores = lax.dot_general(
            query[row], keyset[row], (((0,), (0,)), ((), ())), preferred_element_type=jnp.float32
        )
        scores = scores * DH ** (-0.5) + wide
        weights = jnp.exp(scores - jnp.max(scores, axis=-1, keepdims=True))
        probs = weights * (1.0 / jnp.sum(weights, axis=-1, keepdims=True))
        low = probs.astype(jnp.bfloat16)
        probs_low[row] = low
        dprobs = lax.dot_general(
            cotangent[row], values[row], (((0,), (0,)), ((), ())), preferred_element_type=jnp.float32
        )
        delta = jnp.sum(low.astype(jnp.float32) * dprobs, axis=-1, keepdims=True)
        dscores = probs * (dprobs - delta)
        dscores_low[row] = dscores.astype(jnp.bfloat16)
        summed = dscores if summed is None else summed + dscores
    total[...] = summed.astype(jnp.bfloat16)


def score_grads(query, keyset, values, cotangent, bias):
    rows, depth, width = query.shape
    block = pl.BlockSpec((rows, depth, TILE), lambda j: (0, 0, j))
    whole = pl.BlockSpec((rows, depth, width), lambda j: (0, 0, 0))
    flat = pl.BlockSpec((TILE, width), lambda j: (j, 0))
    tall = pl.BlockSpec((rows, TILE, width), lambda j: (0, j, 0))
    square = jax.ShapeDtypeStruct((rows, width, width), jnp.bfloat16)
    return pl.pallas_call(
        scores_kernel,
        grid=(width // TILE,),
        in_specs=[block, whole, whole, block, flat],
        out_specs=[flat, tall, tall],
        out_shape=[jax.ShapeDtypeStruct((width, width), jnp.bfloat16), square, square],
        compiler_params=pltpu.CompilerParams(vmem_limit_bytes=LIMIT),
        name="score_grads",
    )(query, keyset, values, cotangent, bias)


def inputs_kernel(query, keyset, cotangent, probs_low, dscores_low, grad_q, grad_k, grad_v):
    scale = DH ** (-0.5)
    dscores = dscores_low[...]
    grad_q[...] = (
        lax.dot_general(
            keyset[...], dscores, (((1,), (1,)), ((), ())), preferred_element_type=jnp.float32
        )
        * scale
    ).astype(jnp.bfloat16)
    grad_k[...] = (
        jnp.dot(query[...], dscores, preferred_element_type=jnp.float32) * scale
    ).astype(jnp.bfloat16)
    grad_v[...] = jnp.dot(
        cotangent[...], probs_low[...], preferred_element_type=jnp.float32
    ).astype(jnp.bfloat16)


def input_grads(query, keyset, cotangent, probs_low, dscores_low):
    rows, depth, width = query.shape
    thin = pl.BlockSpec((None, depth, width), lambda i: (i, 0, 0))
    square = pl.BlockSpec((None, width, width), lambda i: (i, 0, 0))
    shape = jax.ShapeDtypeStruct(query.shape, jnp.bfloat16)
    return pl.pallas_call(
        inputs_kernel,
        grid=(rows,),
        in_specs=[thin, thin, thin, square, square],
        out_specs=[thin, thin, thin],
        out_shape=[shape, shape, shape],
        compiler_params=pltpu.CompilerParams(vmem_limit_bytes=LIMIT),
        cost_estimate=pl.CostEstimate(
            flops=6 * rows * depth * width * width, bytes_accessed=8 << 20, transcendentals=0
        ),
        name="input_grads",
    )(query, keyset, cotangent, probs_low, dscores_low)


def exchange(blocks, axes):
    return lax.all_to_all(blocks, axes, 0, 0, tiled=True)


def shards(query, keyset, values, cotangent, pair_norm, bias_weight):
    ny, nz, nx = lax.axis_size("y"), lax.axis_size("z"), lax.axis_size("xh")
    nh = lax.axis_size(HEAD)
    rows, width = pair_norm.shape[1:]
    partial = jnp.einsum("ch,cjk->hjk", bias_weight, pair_norm, preferred_element_type=jnp.float32)
    sent = jnp.broadcast_to(partial[None], (nx, nh, rows, width)).reshape(nx * nh, rows, width)
    parts = exchange(sent, RING).reshape(nx, nh, rows, width)
    own = jnp.sum(parts, axis=1).astype(jnp.bfloat16).reshape(nx * rows, width)
    plane = exchange(jnp.broadcast_to(own[None], (nz,) + own.shape), "z")
    plane = plane.reshape(nz * nx * rows, width)
    full = exchange(jnp.broadcast_to(plane[None], (ny,) + plane.shape), "y")
    full = full.reshape(ny * nz * nx * rows, width)

    query, keyset, values, cotangent = query[0], keyset[0], values[0], cotangent[0]
    total, probs_low, dscores_low = score_grads(query, keyset, values, cotangent, full)
    grad_q, grad_k, grad_v = input_grads(query, keyset, cotangent, probs_low, dscores_low)

    plane = exchange(total.reshape(ny, nz * nx * rows, width), "y")
    plane = jnp.sum(plane.astype(jnp.float32), axis=0).astype(jnp.bfloat16)
    plane = exchange(plane.reshape(nz, nx * rows, width), "z")
    own = jnp.sum(plane.astype(jnp.float32), axis=0).reshape(nx, 1, rows, width)
    sent = jnp.broadcast_to(own, (nx, nh, rows, width)).reshape(nx * nh, rows, width)
    every_head = jnp.sum(exchange(sent, RING).reshape(nx, nh, rows, width), axis=0)
    grad_pair = jnp.einsum(
        "ch,hjk->cjk", bias_weight.astype(jnp.float32), every_head, precision=lax.Precision.HIGHEST
    )
    return grad_q[None], grad_k[None], grad_v[None], grad_pair


def solution(mesh):
    fine = Mesh(mesh.devices.reshape(4, 16, 2, 2, 2), BLK + HEAD)
    four = P(HEAD, BLK, None, None)
    three = P(HEAD, BLK, None)
    return jax.shard_map(
        shards,
        mesh=fine,
        in_specs=(four, four, four, four, three, P(HEAD, None)),
        out_specs=(four, four, four, three),
        check_vma=False,
    )
```

```python
import math

import jax
import jax.numpy as jnp
from jax import lax
from jax.experimental import pallas as pl
from jax.experimental.pallas import tpu as pltpu
from jax.sharding import Mesh
from jax.sharding import PartitionSpec as P

DH = 32
BLK = ("y", "z", "xh")
HEAD = ("xl", "core")
PLANE = ("y", "xh")
LIMIT = 24 * 1024 * 1024
LOG2E = math.log2(math.e)
OUTER = (((0,), (0,)), ((), ()))


def first_half(shape):
    return lax.broadcasted_iota(jnp.int32, shape, 1) < shape[1] // 2


def interleave(low, high):
    half = first_half(low.shape)
    even = jnp.where(half, low, pltpu.roll(high, 4, 1))
    odd = jnp.where(half, pltpu.roll(low, 4, 1), high)
    return jnp.stack([even, odd], axis=1).reshape(-1, low.shape[-1])


def separate(rows):
    pairs = rows.reshape(-1, 2, 8, rows.shape[-1])
    even, odd = pairs[:, 0], pairs[:, 1]
    half = first_half(even.shape)
    low = jnp.where(half, even, pltpu.roll(odd, 4, 1))
    high = jnp.where(half, pltpu.roll(even, 4, 1), odd)
    return low.reshape(-1, rows.shape[-1]), high.reshape(-1, rows.shape[-1])


def bias_tile(bias):
    wide = bias[...].astype(jnp.float32) * LOG2E
    wide = wide.reshape(2, -1, 8, wide.shape[-1])
    return interleave(wide[0], wide[1])


def softmax_parts(query, keyset, wide):
    scores = lax.dot_general(query, keyset, OUTER, preferred_element_type=jnp.float32)
    scores = scores * (LOG2E * DH ** (-0.5)) + wide
    weights = jnp.exp2(scores - jnp.max(scores, axis=-1, keepdims=True))
    return weights, 1.0 / jnp.sum(weights, axis=-1, keepdims=True)


def sum_kernel(query, keyset, values, cotangent, bias, total):
    wide = bias_tile(bias)
    summed = None
    for row in range(query.shape[0]):
        weights, inverse = softmax_parts(query[row], keyset[row], wide)
        dprobs = lax.dot_general(
            cotangent[row], values[row], OUTER, preferred_element_type=jnp.float32
        )
        delta = jnp.sum(weights * dprobs, axis=-1, keepdims=True) * inverse
        dscores = (weights * inverse) * (dprobs - delta)
        summed = dscores if summed is None else summed + dscores
    low, high = separate(summed)
    total[0] = low.astype(jnp.bfloat16)
    total[1] = high.astype(jnp.bfloat16)


def inputs_kernel(query, keyset, values, cotangent, bias, grad_q, grad_k, grad_v, sum_k, sum_v):
    step = pl.program_id(0)
    wide = bias_tile(bias)

    @pl.when(step == 0)
    def _():
        sum_k[...] = jnp.zeros_like(sum_k)
        sum_v[...] = jnp.zeros_like(sum_v)

    for row in range(query.shape[0]):
        weights, inverse = softmax_parts(query[row], keyset[row], wide)
        probs = weights * inverse
        low = probs.astype(jnp.bfloat16)
        dprobs = lax.dot_general(
            cotangent[row], values[row], OUTER, preferred_element_type=jnp.float32
        )
        delta = jnp.sum(low.astype(jnp.float32) * dprobs, axis=-1, keepdims=True)
        dscores = (probs * (dprobs - delta)).astype(jnp.bfloat16)
        sum_k[row] += jnp.dot(query[row], dscores, preferred_element_type=jnp.float32)
        sum_v[row] += jnp.dot(cotangent[row], low, preferred_element_type=jnp.float32)
        turned = lax.dot_general(
            keyset[row], dscores, (((1,), (1,)), ((), ())), preferred_element_type=jnp.float32
        )
        grad_q[row] = (turned * DH ** (-0.5)).astype(jnp.bfloat16)

    @pl.when(step == pl.num_programs(0) - 1)
    def _():
        grad_k[...] = (sum_k[...] * DH ** (-0.5)).astype(jnp.bfloat16)
        grad_v[...] = sum_v[...].astype(jnp.bfloat16)


def specs(query, bias):
    rows, depth, width = query.shape
    tiles = bias.shape[0] // 2
    block = pl.BlockSpec((rows, depth, width // tiles), lambda j: (0, 0, j))
    whole = pl.BlockSpec((rows, depth, width), lambda j: (0, 0, 0))
    pair = pl.BlockSpec((2,) + bias.shape[1:], lambda j: (j, 0, 0))
    return tiles, block, whole, pair


def bias_sum(query, keyset, values, cotangent, bias):
    tiles, block, whole, pair = specs(query, bias)
    return pl.pallas_call(
        sum_kernel,
        grid=(tiles,),
        in_specs=[block, whole, whole, block, pair],
        out_specs=pair,
        out_shape=jax.ShapeDtypeStruct(bias.shape, jnp.bfloat16),
        compiler_params=pltpu.CompilerParams(vmem_limit_bytes=LIMIT),
        name="bias_sum",
    )(query, keyset, values, cotangent, bias)


def input_grads(query, keyset, values, cotangent, bias):
    tiles, block, whole, pair = specs(query, bias)
    rows, depth, width = query.shape
    shape = jax.ShapeDtypeStruct(query.shape, jnp.bfloat16)
    return pl.pallas_call(
        inputs_kernel,
        grid=(tiles,),
        in_specs=[block, whole, whole, block, pair],
        out_specs=[block, whole, whole],
        out_shape=[shape] * 3,
        scratch_shapes=[pltpu.VMEM(query.shape, jnp.float32)] * 2,
        compiler_params=pltpu.CompilerParams(vmem_limit_bytes=LIMIT),
        cost_estimate=pl.CostEstimate(
            flops=10 * rows * depth * width * width,
            bytes_accessed=1 << 20,
            transcendentals=rows * width * width,
        ),
        name="input_grads",
    )(query, keyset, values, cotangent, bias)


def pair_kernel(weight, every_head, grad_pair):
    cores, pairs = every_head.shape[:2]
    for head in range(pairs * cores):
        scale = weight[:, head : head + 1].astype(jnp.float32)[:, :, None]
        term = scale * every_head[head % cores, head // cores][None]
        if head == 0:
            grad_pair[...] = term
        else:
            grad_pair[...] += term


def pair_grad(weight, every_head):
    held = pl.BlockSpec(memory_space=pltpu.VMEM)
    return pl.pallas_call(
        pair_kernel,
        in_specs=[held, held],
        out_specs=held,
        out_shape=jax.ShapeDtypeStruct(weight.shape[:1] + every_head.shape[2:], jnp.float32),
        compiler_params=pltpu.CompilerParams(vmem_limit_bytes=LIMIT),
        name="pair_grad",
    )(weight, every_head)


def exchange(blocks, axes):
    return lax.all_to_all(blocks, axes, 0, 0, tiled=True)


def shards(query, keyset, values, cotangent, pair_norm, bias_weight):
    nz = lax.axis_size("z")
    planes = lax.axis_size(PLANE)
    rows, width = pair_norm.shape[1:]
    query, keyset, values, cotangent = query[0], keyset[0], values[0], cotangent[0]

    partial = jnp.einsum("ch,cjk->hjk", bias_weight, pair_norm, preferred_element_type=jnp.float32)
    own = jnp.sum(exchange(partial, HEAD), axis=0).astype(jnp.bfloat16)
    line = exchange(jnp.broadcast_to(own[None], (nz, rows, width)), "z").reshape(nz * rows, width)
    bias = exchange(jnp.broadcast_to(line[None], (planes,) + line.shape), PLANE)

    total = bias_sum(query, keyset, values, cotangent, bias)
    line = jnp.sum(exchange(total, PLANE).astype(jnp.float32), axis=0).astype(jnp.bfloat16)
    pairs = lax.axis_size("xl")
    line = jnp.broadcast_to(line.reshape(nz, 1, rows, width), (nz, pairs, rows, width))
    line = exchange(line.reshape(nz * pairs, rows, width), ("z", "xl"))
    grads = input_grads(query, keyset, values, cotangent, bias)
    line, *grads = lax.optimization_barrier((line, *grads))
    own = jnp.sum(line.astype(jnp.float32).reshape(nz, pairs, rows, width), axis=0)
    every_head = lax.all_gather(own, "core", axis=0)
    grad_pair = pair_grad(bias_weight, every_head)
    return grads[0][None], grads[1][None], grads[2][None], grad_pair


def solution(mesh):
    fine = Mesh(mesh.devices.reshape(4, 16, 2, 2, 2), BLK + HEAD)
    four = P(HEAD, BLK, None, None)
    three = P(HEAD, BLK, None)
    return jax.shard_map(
        shards,
        mesh=fine,
        in_specs=(four, four, four, four, three, P(HEAD, None)),
        out_specs=(four, four, four, three),
        check_vma=False,
    )
```

```python
import math

import jax
import jax.numpy as jnp
from jax import lax
from jax.experimental import pallas as pl
from jax.experimental.pallas import tpu as pltpu
from jax.sharding import Mesh
from jax.sharding import PartitionSpec as P

DH = 32
BLK = ("y", "z", "xh")
HEAD = ("xl", "core")
PLANE = ("y", "xh")
PLANE_ORDER = (5, 4, 7, 6, 1, 0, 3, 2)


def middle_first(count):
    return [(i + count // 2) % count for i in range(count)]


def place(y, xh):
    return PLANE_ORDER.index(2 * y + xh)


LIMIT = 24 * 1024 * 1024
LOG2E = math.log2(math.e)
OUTER = (((0,), (0,)), ((), ()))


def first_half(shape):
    return lax.broadcasted_iota(jnp.int32, shape, 1) < shape[1] // 2


def interleave(low, high):
    half = first_half(low.shape)
    even = jnp.where(half, low, pltpu.roll(high, 4, 1))
    odd = jnp.where(half, pltpu.roll(low, 4, 1), high)
    return jnp.stack([even, odd], axis=1).reshape(-1, low.shape[-1])


def separate(rows):
    pairs = rows.reshape(-1, 2, 8, rows.shape[-1])
    even, odd = pairs[:, 0], pairs[:, 1]
    half = first_half(even.shape)
    low = jnp.where(half, even, pltpu.roll(odd, 4, 1))
    high = jnp.where(half, pltpu.roll(even, 4, 1), odd)
    return low.reshape(-1, rows.shape[-1]), high.reshape(-1, rows.shape[-1])


def turned(rows):
    half = rows.shape[0] // 2
    return jnp.concatenate([rows[half:], rows[:half]], axis=0)


def bias_tile(bias, tile):
    low, high = (
        (bias[place(tile, part)].astype(jnp.float32) * LOG2E).reshape(-1, 8, bias.shape[-1])
        for part in range(2)
    )
    return turned(interleave(low, high))


def softmax_parts(query, keyset, wide):
    scores = lax.dot_general(query, keyset, OUTER, preferred_element_type=jnp.float32)
    scores = scores * (LOG2E * DH ** (-0.5)) + wide
    weights = jnp.exp2(scores - jnp.max(scores, axis=-1, keepdims=True))
    return weights, 1.0 / jnp.sum(weights, axis=-1, keepdims=True)


def sum_kernel(query, keyset, values, cotangent, bias, total):
    own = 2 * bias.shape[1]
    for tile in range(bias.shape[0] // 2):
        columns = slice(tile * own, (tile + 1) * own)
        wide = bias_tile(bias, tile)
        summed = None
        for row in range(query.shape[0]):
            weights, inverse = softmax_parts(query[row, :, columns], keyset[row], wide)
            dprobs = lax.dot_general(
                cotangent[row, :, columns], values[row], OUTER, preferred_element_type=jnp.float32
            )
            delta = jnp.sum(weights * dprobs, axis=-1, keepdims=True) * inverse
            dscores = (weights * inverse) * (dprobs - delta)
            summed = dscores if summed is None else summed + dscores
        for part, half in enumerate(separate(turned(summed))):
            total[place(tile, part)] = half.astype(jnp.bfloat16)


def bias_sum(query, keyset, values, cotangent, bias):
    held = pl.BlockSpec(memory_space=pltpu.VMEM)
    return pl.pallas_call(
        sum_kernel,
        in_specs=[held] * 5,
        out_specs=held,
        out_shape=jax.ShapeDtypeStruct(bias.shape, jnp.bfloat16),
        compiler_params=pltpu.CompilerParams(vmem_limit_bytes=LIMIT),
        name="bias_sum",
    )(query, keyset, values, cotangent, bias)


def inputs_kernel(query, keyset, values, cotangent, bias, *refs):
    grad_q, grad_k, grad_v, probs_low, dscores_low = refs
    own = 2 * bias.shape[1]
    scale = DH ** (-0.5)
    for row in range(query.shape[0]):
        for tile in range(bias.shape[0] // 2):
            columns = slice(tile * own, (tile + 1) * own)
            wide = bias_tile(bias, tile)
            weights, inverse = softmax_parts(query[row, :, columns], keyset[row], wide)
            probs = weights * inverse
            low = probs.astype(jnp.bfloat16)
            dprobs = lax.dot_general(
                cotangent[row, :, columns], values[row], OUTER, preferred_element_type=jnp.float32
            )
            delta = jnp.sum(low.astype(jnp.float32) * dprobs, axis=-1, keepdims=True)
            probs_low[row, columns] = low
            dscores_low[row, columns] = (probs * (dprobs - delta)).astype(jnp.bfloat16)
    for row in range(query.shape[0]):
        dscores = dscores_low[row]
        turned = lax.dot_general(
            keyset[row], dscores, (((1,), (1,)), ((), ())), preferred_element_type=jnp.float32
        )
        grad_q[row] = (turned * scale).astype(jnp.bfloat16)
        product = jnp.dot(query[row], dscores, preferred_element_type=jnp.float32)
        grad_k[row] = (product * scale).astype(jnp.bfloat16)
        grad_v[row] = jnp.dot(
            cotangent[row], probs_low[row], preferred_element_type=jnp.float32
        ).astype(jnp.bfloat16)


def input_grads(query, keyset, values, cotangent, bias):
    rows, depth, width = query.shape
    held = pl.BlockSpec(memory_space=pltpu.VMEM)
    whole = pl.BlockSpec(query.shape, lambda i: (0, 0, 0))
    shape = jax.ShapeDtypeStruct(query.shape, jnp.bfloat16)
    return pl.pallas_call(
        inputs_kernel,
        grid=(1,),
        in_specs=[held] * 5,
        out_specs=[whole] * 3,
        out_shape=[shape] * 3,
        scratch_shapes=[pltpu.VMEM((rows, width, width), jnp.bfloat16)] * 2,
        compiler_params=pltpu.CompilerParams(vmem_limit_bytes=LIMIT),
        cost_estimate=pl.CostEstimate(
            flops=10 * rows * depth * width * width,
            bytes_accessed=1 << 20,
            transcendentals=rows * width * width,
        ),
        name="input_grads",
    )(query, keyset, values, cotangent, bias)


def pair_kernel(weight, every_head, grad_pair):
    for head in range(every_head.shape[0]):
        scale = weight[:, head : head + 1].astype(jnp.float32)[:, :, None]
        term = scale * every_head[head][None]
        if head == 0:
            grad_pair[...] = term
        else:
            grad_pair[...] += term


def pair_grad(weight, every_head):
    held = pl.BlockSpec(memory_space=pltpu.VMEM)
    return pl.pallas_call(
        pair_kernel,
        in_specs=[held, held],
        out_specs=held,
        out_shape=jax.ShapeDtypeStruct(weight.shape[:1] + every_head.shape[1:], jnp.float32),
        compiler_params=pltpu.CompilerParams(vmem_limit_bytes=LIMIT),
        name="pair_grad",
    )(weight, every_head)


def exchange(blocks, axes, order=None):
    groups = None if order is None else [list(order)]
    return lax.all_to_all(blocks, axes, 0, 0, axis_index_groups=groups, tiled=True)


def shards(query, keyset, values, cotangent, pair_norm, bias_weight):
    nz = lax.axis_size("z")
    rows, width = pair_norm.shape[1:]
    query, keyset, values, cotangent = query[0], keyset[0], values[0], cotangent[0]

    partial = jnp.einsum("ch,cjk->hjk", bias_weight, pair_norm, preferred_element_type=jnp.float32)
    own = jnp.sum(exchange(partial, HEAD), axis=0).astype(jnp.bfloat16)
    line = jnp.broadcast_to(own[None], (nz, rows, width))
    line = exchange(line, "z", middle_first(nz)).reshape(nz * rows, width)
    planes = lax.axis_size(PLANE)
    bias = exchange(jnp.broadcast_to(line[None], (planes,) + line.shape), PLANE, PLANE_ORDER)

    total = bias_sum(query, keyset, values, cotangent, bias)
    line = jnp.sum(exchange(total, PLANE, PLANE_ORDER).astype(jnp.float32), axis=0).astype(jnp.bfloat16)
    line = exchange(line.reshape(nz, rows, width), "z", middle_first(nz))
    grads = input_grads(query, keyset, values, cotangent, bias)
    line, *grads = lax.optimization_barrier((line, *grads))
    own = jnp.sum(line.astype(jnp.float32), axis=0)
    every_head = lax.all_gather(own, HEAD, axis=0)
    grad_pair = pair_grad(bias_weight, every_head)
    return grads[0][None], grads[1][None], grads[2][None], grad_pair


def solution(mesh):
    fine = Mesh(mesh.devices.reshape(4, 16, 2, 2, 2), BLK + HEAD)
    four = P(HEAD, BLK, None, None)
    three = P(HEAD, BLK, None)
    return jax.shard_map(
        shards,
        mesh=fine,
        in_specs=(four, four, four, four, three, P(HEAD, None)),
        out_specs=(four, four, four, three),
        check_vma=False,
    )
```

```python
import math

import jax
import jax.numpy as jnp
from jax import lax
from jax.experimental import pallas as pl
from jax.experimental.pallas import tpu as pltpu
from jax.sharding import Mesh
from jax.sharding import PartitionSpec as P

DH = 32
BLK = ("y", "z", "xh")
HEAD = ("xl", "core")
PLANE = ("y", "xh")
PLANE_ORDER = (5, 4, 7, 6, 1, 0, 3, 2)


def middle_first(count):
    return [(i + count // 2) % count for i in range(count)]


def place(y, xh):
    return PLANE_ORDER.index(2 * y + xh)


LIMIT = 24 * 1024 * 1024
LOG2E = math.log2(math.e)
OUTER = (((0,), (0,)), ((), ()))


def first_half(shape):
    return lax.broadcasted_iota(jnp.int32, shape, 1) < shape[1] // 2


def interleave(low, high):
    half = first_half(low.shape)
    even = jnp.where(half, low, pltpu.roll(high, 4, 1))
    odd = jnp.where(half, pltpu.roll(low, 4, 1), high)
    return jnp.stack([even, odd], axis=1).reshape(-1, low.shape[-1])


def separate(rows):
    pairs = rows.reshape(-1, 2, 8, rows.shape[-1])
    even, odd = pairs[:, 0], pairs[:, 1]
    half = first_half(even.shape)
    low = jnp.where(half, even, pltpu.roll(odd, 4, 1))
    high = jnp.where(half, pltpu.roll(even, 4, 1), odd)
    return low.reshape(-1, rows.shape[-1]), high.reshape(-1, rows.shape[-1])


def turned(rows):
    half = rows.shape[0] // 2
    return jnp.concatenate([rows[half:], rows[:half]], axis=0)


def bias_tile(bias, tile):
    low, high = (
        (bias[place(tile, part)].astype(jnp.float32) * LOG2E).reshape(-1, 8, bias.shape[-1])
        for part in range(2)
    )
    return turned(interleave(low, high))


def softmax_parts(query, keyset, wide):
    scores = lax.dot_general(query, keyset, OUTER, preferred_element_type=jnp.float32)
    scores = scores * (LOG2E * DH ** (-0.5)) + wide
    weights = jnp.exp2(scores - jnp.max(scores, axis=-1, keepdims=True))
    return weights, 1.0 / jnp.sum(weights, axis=-1, keepdims=True)


def sum_kernel(query, keyset, values, cotangent, bias, total):
    own = 2 * bias.shape[1]
    for tile in range(bias.shape[0] // 2):
        columns = slice(tile * own, (tile + 1) * own)
        wide = bias_tile(bias, tile)
        summed = None
        for row in range(query.shape[0]):
            weights, inverse = softmax_parts(query[row, :, columns], keyset[row], wide)
            dprobs = lax.dot_general(
                cotangent[row, :, columns], values[row], OUTER, preferred_element_type=jnp.float32
            )
            delta = jnp.sum(weights * dprobs, axis=-1, keepdims=True) * inverse
            dscores = (weights * inverse) * (dprobs - delta)
            summed = dscores if summed is None else summed + dscores
        for part, half in enumerate(separate(turned(summed))):
            total[place(tile, part)] = half.astype(jnp.bfloat16)


def bias_sum(query, keyset, values, cotangent, bias):
    held = pl.BlockSpec(memory_space=pltpu.VMEM)
    return pl.pallas_call(
        sum_kernel,
        in_specs=[held] * 5,
        out_specs=held,
        out_shape=jax.ShapeDtypeStruct(bias.shape, jnp.bfloat16),
        compiler_params=pltpu.CompilerParams(vmem_limit_bytes=LIMIT),
        name="bias_sum",
    )(query, keyset, values, cotangent, bias)


def inputs_kernel(query, keyset, values, cotangent, bias, *refs):
    grad_q, grad_k, grad_v, probs_low, dscores_low = refs
    own = 2 * bias.shape[1]
    scale = DH ** (-0.5)
    for row in range(query.shape[0]):
        for tile in range(bias.shape[0] // 2):
            columns = slice(tile * own, (tile + 1) * own)
            wide = bias_tile(bias, tile)
            weights, inverse = softmax_parts(query[row, :, columns], keyset[row], wide)
            probs = weights * inverse
            low = probs.astype(jnp.bfloat16)
            dprobs = lax.dot_general(
                cotangent[row, :, columns], values[row], OUTER, preferred_element_type=jnp.float32
            )
            delta = jnp.sum(low.astype(jnp.float32) * dprobs, axis=-1, keepdims=True)
            probs_low[row, columns] = low
            dscores_low[row, columns] = (probs * (dprobs - delta)).astype(jnp.bfloat16)
    for row in range(query.shape[0]):
        dscores = dscores_low[row]
        turned = lax.dot_general(
            keyset[row], dscores, (((1,), (1,)), ((), ())), preferred_element_type=jnp.float32
        )
        grad_q[row] = (turned * scale).astype(jnp.bfloat16)
        product = jnp.dot(query[row], dscores, preferred_element_type=jnp.float32)
        grad_k[row] = (product * scale).astype(jnp.bfloat16)
        grad_v[row] = jnp.dot(
            cotangent[row], probs_low[row], preferred_element_type=jnp.float32
        ).astype(jnp.bfloat16)


def input_grads(query, keyset, values, cotangent, bias):
    rows, depth, width = query.shape
    held = pl.BlockSpec(memory_space=pltpu.VMEM)
    whole = pl.BlockSpec(query.shape, lambda i: (0, 0, 0))
    shape = jax.ShapeDtypeStruct(query.shape, jnp.bfloat16)
    return pl.pallas_call(
        inputs_kernel,
        grid=(1,),
        in_specs=[held] * 5,
        out_specs=[whole] * 3,
        out_shape=[shape] * 3,
        scratch_shapes=[pltpu.VMEM((rows, width, width), jnp.bfloat16)] * 2,
        compiler_params=pltpu.CompilerParams(vmem_limit_bytes=LIMIT),
        cost_estimate=pl.CostEstimate(
            flops=10 * rows * depth * width * width,
            bytes_accessed=1 << 20,
            transcendentals=rows * width * width,
        ),
        name="input_grads",
    )(query, keyset, values, cotangent, bias)


def pair_kernel(weight, every_head, grad_pair):
    for head in range(4):
        scale = weight[:, head : head + 1].astype(jnp.float32)[:, :, None]
        term = scale * every_head[head % 2, 1 - head // 2][None]
        if head == 0:
            grad_pair[...] = term
        else:
            grad_pair[...] += term


def pair_grad(weight, every_head):
    held = pl.BlockSpec(memory_space=pltpu.VMEM)
    return pl.pallas_call(
        pair_kernel,
        in_specs=[held, held],
        out_specs=held,
        out_shape=jax.ShapeDtypeStruct(weight.shape[:1] + every_head.shape[2:], jnp.float32),
        compiler_params=pltpu.CompilerParams(vmem_limit_bytes=LIMIT),
        name="pair_grad",
    )(weight, every_head)


def exchange(blocks, axes, order=None):
    groups = None if order is None else [list(order)]
    return lax.all_to_all(blocks, axes, 0, 0, axis_index_groups=groups, tiled=True)


def shards(query, keyset, values, cotangent, pair_norm, bias_weight):
    nz = lax.axis_size("z")
    rows, width = pair_norm.shape[1:]
    query, keyset, values, cotangent = query[0], keyset[0], values[0], cotangent[0]

    partial = jnp.einsum("ch,cjk->hjk", bias_weight, pair_norm, preferred_element_type=jnp.float32)
    own = jnp.sum(exchange(partial, HEAD), axis=0).astype(jnp.bfloat16)
    line = jnp.broadcast_to(own[None], (nz, rows, width))
    line = exchange(line, "z", middle_first(nz)).reshape(nz * rows, width)
    planes = lax.axis_size(PLANE)
    bias = exchange(jnp.broadcast_to(line[None], (planes,) + line.shape), PLANE, PLANE_ORDER)

    total = bias_sum(query, keyset, values, cotangent, bias)
    line = jnp.sum(exchange(total, PLANE, PLANE_ORDER).astype(jnp.float32), axis=0).astype(jnp.bfloat16)
    line = jnp.broadcast_to(line.reshape(nz, 1, rows, width), (nz, 2, rows, width))
    order = [2 * z + xl for z in middle_first(nz) for xl in (1, 0)]
    line = exchange(line.reshape(nz * 2, rows, width), ("z", "xl"), order)
    grads = input_grads(query, keyset, values, cotangent, bias)
    line, *grads = lax.optimization_barrier((line, *grads))
    own = jnp.sum(line.astype(jnp.float32).reshape(nz, 2, rows, width), axis=0)
    every_head = lax.all_gather(own, "core", axis=0)
    grad_pair = pair_grad(bias_weight, every_head)
    return grads[0][None], grads[1][None], grads[2][None], grad_pair


def solution(mesh):
    fine = Mesh(mesh.devices.reshape(4, 16, 2, 2, 2), BLK + HEAD)
    four = P(HEAD, BLK, None, None)
    three = P(HEAD, BLK, None)
    return jax.shard_map(
        shards,
        mesh=fine,
        in_specs=(four, four, four, four, three, P(HEAD, None)),
        out_specs=(four, four, four, three),
        check_vma=False,
    )
```

```python
import math

import jax
import jax.numpy as jnp
from jax import lax
from jax.experimental import pallas as pl
from jax.experimental.pallas import tpu as pltpu
from jax.sharding import Mesh
from jax.sharding import PartitionSpec as P

DH = 32
BLK = ("y", "z", "xh")
HEAD = ("xl", "core")
PLANE = ("y", "xh")
PLANE_ORDER = (5, 4, 7, 6, 1, 0, 3, 2)


def middle_first(count):
    return [(i + count // 2) % count for i in range(count)]


def place(y, xh):
    return PLANE_ORDER.index(2 * y + xh)


LIMIT = 24 * 1024 * 1024
LOG2E = math.log2(math.e)
OUTER = (((0,), (0,)), ((), ()))


def first_half(shape):
    return lax.broadcasted_iota(jnp.int32, shape, 1) < shape[1] // 2


def interleave(low, high):
    half = first_half(low.shape)
    even = jnp.where(half, low, pltpu.roll(high, 4, 1))
    odd = jnp.where(half, pltpu.roll(low, 4, 1), high)
    return jnp.stack([even, odd], axis=1).reshape(-1, low.shape[-1])


def separate(rows):
    pairs = rows.reshape(-1, 2, 8, rows.shape[-1])
    even, odd = pairs[:, 0], pairs[:, 1]
    half = first_half(even.shape)
    low = jnp.where(half, even, pltpu.roll(odd, 4, 1))
    high = jnp.where(half, pltpu.roll(even, 4, 1), odd)
    return low.reshape(-1, rows.shape[-1]), high.reshape(-1, rows.shape[-1])


def turned(rows):
    half = rows.shape[0] // 2
    return jnp.concatenate([rows[half:], rows[:half]], axis=0)


def bias_tile(bias, tile):
    low, high = (
        (bias[place(tile, part)].astype(jnp.float32) * LOG2E).reshape(-1, 8, bias.shape[-1])
        for part in range(2)
    )
    return turned(interleave(low, high))


def softmax_parts(query, keyset, wide):
    scores = lax.dot_general(query, keyset, OUTER, preferred_element_type=jnp.float32)
    scores = scores * (LOG2E * DH ** (-0.5)) + wide
    weights = jnp.exp2(scores - jnp.max(scores, axis=-1, keepdims=True))
    return weights, 1.0 / jnp.sum(weights, axis=-1, keepdims=True)


def sum_kernel(query, keyset, values, cotangent, bias, total):
    own = 2 * bias.shape[1]
    for pair in range(bias.shape[0] // 4):
        tiles = (2 * pair, 2 * pair + 1)
        columns = slice(tiles[0] * own, (tiles[1] + 1) * own)
        wide = jnp.concatenate([bias_tile(bias, tile) for tile in tiles], axis=0)
        summed = None
        for row in range(query.shape[0]):
            weights, inverse = softmax_parts(query[row, :, columns], keyset[row], wide)
            dprobs = lax.dot_general(
                cotangent[row, :, columns], values[row], OUTER, preferred_element_type=jnp.float32
            )
            delta = jnp.sum(weights * dprobs, axis=-1, keepdims=True) * inverse
            dscores = (weights * inverse) * (dprobs - delta)
            summed = dscores if summed is None else summed + dscores
        for index, tile in enumerate(tiles):
            rows = summed[index * own : (index + 1) * own]
            for part, half in enumerate(separate(turned(rows))):
                total[place(tile, part)] = half.astype(jnp.bfloat16)


def bias_sum(query, keyset, values, cotangent, bias):
    held = pl.BlockSpec(memory_space=pltpu.VMEM)
    return pl.pallas_call(
        sum_kernel,
        in_specs=[held] * 5,
        out_specs=held,
        out_shape=jax.ShapeDtypeStruct(bias.shape, jnp.bfloat16),
        compiler_params=pltpu.CompilerParams(vmem_limit_bytes=LIMIT),
        name="bias_sum",
    )(query, keyset, values, cotangent, bias)


def inputs_kernel(query, keyset, values, cotangent, bias, *refs):
    grad_q, grad_k, grad_v, probs_low, dscores_low = refs
    own = 2 * bias.shape[1]
    scale = DH ** (-0.5)
    for row in range(query.shape[0]):
        for tile in range(bias.shape[0] // 2):
            columns = slice(tile * own, (tile + 1) * own)
            wide = bias_tile(bias, tile)
            weights, inverse = softmax_parts(query[row, :, columns], keyset[row], wide)
            probs = weights * inverse
            low = probs.astype(jnp.bfloat16)
            dprobs = lax.dot_general(
                cotangent[row, :, columns], values[row], OUTER, preferred_element_type=jnp.float32
            )
            delta = jnp.sum(low.astype(jnp.float32) * dprobs, axis=-1, keepdims=True)
            probs_low[row, columns] = low
            dscores_low[row, columns] = (probs * (dprobs - delta)).astype(jnp.bfloat16)
    for row in range(query.shape[0]):
        dscores = dscores_low[row]
        turned = lax.dot_general(
            keyset[row], dscores, (((1,), (1,)), ((), ())), preferred_element_type=jnp.float32
        )
        grad_q[row] = (turned * scale).astype(jnp.bfloat16)
        product = jnp.dot(query[row], dscores, preferred_element_type=jnp.float32)
        grad_k[row] = (product * scale).astype(jnp.bfloat16)
        grad_v[row] = jnp.dot(
            cotangent[row], probs_low[row], preferred_element_type=jnp.float32
        ).astype(jnp.bfloat16)


def input_grads(query, keyset, values, cotangent, bias):
    rows, depth, width = query.shape
    held = pl.BlockSpec(memory_space=pltpu.VMEM)
    whole = pl.BlockSpec(query.shape, lambda i: (0, 0, 0))
    shape = jax.ShapeDtypeStruct(query.shape, jnp.bfloat16)
    return pl.pallas_call(
        inputs_kernel,
        grid=(1,),
        in_specs=[held] * 5,
        out_specs=[whole] * 3,
        out_shape=[shape] * 3,
        scratch_shapes=[pltpu.VMEM((rows, width, width), jnp.bfloat16)] * 2,
        compiler_params=pltpu.CompilerParams(vmem_limit_bytes=LIMIT),
        cost_estimate=pl.CostEstimate(
            flops=10 * rows * depth * width * width,
            bytes_accessed=1 << 20,
            transcendentals=rows * width * width,
        ),
        name="input_grads",
    )(query, keyset, values, cotangent, bias)


def fold_kernel(parts, line):
    summed = parts[0].astype(jnp.float32)
    for part in range(1, parts.shape[0]):
        summed = summed + parts[part].astype(jnp.float32)
    rows = line.shape[2]
    for block in range(line.shape[0]):
        low = summed[block * rows : (block + 1) * rows].astype(jnp.bfloat16)
        for copy in range(line.shape[1]):
            line[block, copy] = low


def fold(parts, rows, copies):
    held = pl.BlockSpec(memory_space=pltpu.VMEM)
    shape = (parts.shape[1] // rows, copies, rows, parts.shape[2])
    return pl.pallas_call(
        fold_kernel,
        in_specs=[held],
        out_specs=held,
        out_shape=jax.ShapeDtypeStruct(shape, jnp.bfloat16),
        compiler_params=pltpu.CompilerParams(vmem_limit_bytes=LIMIT),
        name="fold",
    )(parts)


def project_kernel(weight, pair_norm, partial):
    scales = weight[...].astype(jnp.float32)
    wide = pair_norm[...].astype(jnp.float32)
    for head in range(partial.shape[0]):
        partial[head] = jnp.sum(scales[:, head : head + 1][:, :, None] * wide, axis=0)


def project(weight, pair_norm):
    held = pl.BlockSpec(memory_space=pltpu.VMEM)
    return pl.pallas_call(
        project_kernel,
        in_specs=[held, held],
        out_specs=held,
        out_shape=jax.ShapeDtypeStruct(weight.shape[1:] + pair_norm.shape[1:], jnp.float32),
        compiler_params=pltpu.CompilerParams(vmem_limit_bytes=LIMIT),
        name="project",
    )(weight, pair_norm)


def pair_kernel(weight, every_head, grad_pair):
    for head in range(4):
        scale = weight[:, head : head + 1].astype(jnp.float32)[:, :, None]
        term = scale * every_head[head % 2, 1 - head // 2][None]
        if head == 0:
            grad_pair[...] = term
        else:
            grad_pair[...] += term


def pair_grad(weight, every_head):
    held = pl.BlockSpec(memory_space=pltpu.VMEM)
    return pl.pallas_call(
        pair_kernel,
        in_specs=[held, held],
        out_specs=held,
        out_shape=jax.ShapeDtypeStruct(weight.shape[:1] + every_head.shape[2:], jnp.float32),
        compiler_params=pltpu.CompilerParams(vmem_limit_bytes=LIMIT),
        name="pair_grad",
    )(weight, every_head)


def exchange(blocks, axes, order=None):
    groups = None if order is None else [list(order)]
    return lax.all_to_all(blocks, axes, 0, 0, axis_index_groups=groups, tiled=True)


def shards(query, keyset, values, cotangent, pair_norm, bias_weight):
    nz = lax.axis_size("z")
    rows, width = pair_norm.shape[1:]
    query, keyset, values, cotangent = query[0], keyset[0], values[0], cotangent[0]

    partial = jnp.einsum("ch,cjk->hjk", bias_weight, pair_norm, preferred_element_type=jnp.float32)
    own = jnp.sum(exchange(partial, HEAD), axis=0).astype(jnp.bfloat16)
    line = jnp.broadcast_to(own[None], (nz, rows, width))
    line = exchange(line, "z", middle_first(nz)).reshape(nz * rows, width)
    planes = lax.axis_size(PLANE)
    bias = exchange(jnp.broadcast_to(line[None], (planes,) + line.shape), PLANE, PLANE_ORDER)

    total = bias_sum(query, keyset, values, cotangent, bias)
    line = fold(exchange(total, PLANE, PLANE_ORDER), rows, 2)
    order = [2 * z + xl for z in middle_first(nz) for xl in (1, 0)]
    line = exchange(line.reshape(nz * 2, rows, width), ("z", "xl"), order)
    grads = input_grads(query, keyset, values, cotangent, bias)
    line, *grads = lax.optimization_barrier((line, *grads))
    own = jnp.sum(line.astype(jnp.float32).reshape(nz, 2, rows, width), axis=0)
    every_head = lax.all_gather(own, "core", axis=0)
    grad_pair = pair_grad(bias_weight, every_head)
    return grads[0][None], grads[1][None], grads[2][None], grad_pair


def solution(mesh):
    fine = Mesh(mesh.devices.reshape(4, 16, 2, 2, 2), BLK + HEAD)
    four = P(HEAD, BLK, None, None)
    three = P(HEAD, BLK, None)
    return jax.shard_map(
        shards,
        mesh=fine,
        in_specs=(four, four, four, four, three, P(HEAD, None)),
        out_specs=(four, four, four, three),
        check_vma=False,
    )
```

```python
import math

import jax
import jax.numpy as jnp
from jax import lax
from jax.experimental import pallas as pl
from jax.experimental.pallas import tpu as pltpu
from jax.sharding import Mesh
from jax.sharding import PartitionSpec as P

DH = 32
BLK = ("y", "z", "xh")
HEAD = ("xl", "core")
PLANE = ("y", "xh")
FIRST_IN, FIRST_OUT = 10, 10
PLANE_ORDER = (5, 4, 7, 6, 1, 0, 3, 2)


def starting(first, count):
    return [(first + i) % count for i in range(count)]


def place(y, xh):
    return PLANE_ORDER.index(2 * y + xh)


LIMIT = 24 * 1024 * 1024
LOG2E = math.log2(math.e)
OUTER = (((0,), (0,)), ((), ()))


def first_half(shape):
    return lax.broadcasted_iota(jnp.int32, shape, 1) < shape[1] // 2


def interleave(low, high):
    half = first_half(low.shape)
    even = jnp.where(half, low, pltpu.roll(high, 4, 1))
    odd = jnp.where(half, pltpu.roll(low, 4, 1), high)
    return jnp.stack([even, odd], axis=1).reshape(-1, low.shape[-1])


def separate(rows):
    pairs = rows.reshape(-1, 2, 8, rows.shape[-1])
    even, odd = pairs[:, 0], pairs[:, 1]
    half = first_half(even.shape)
    low = jnp.where(half, even, pltpu.roll(odd, 4, 1))
    high = jnp.where(half, pltpu.roll(even, 4, 1), odd)
    return low.reshape(-1, rows.shape[-1]), high.reshape(-1, rows.shape[-1])


def rolled(rows, blocks):
    cut = 8 * blocks % rows.shape[0]
    return jnp.concatenate([rows[cut:], rows[:cut]], axis=0) if cut else rows


def bias_tile(bias, tile):
    low, high = (
        (bias[place(tile, part)].astype(jnp.float32) * LOG2E).reshape(-1, 8, bias.shape[-1])
        for part in range(2)
    )
    return rolled(interleave(low, high), -FIRST_IN)


def softmax_parts(query, keyset, wide):
    scores = lax.dot_general(query, keyset, OUTER, preferred_element_type=jnp.float32)
    scores = scores * (LOG2E * DH ** (-0.5)) + wide
    weights = jnp.exp2(scores - jnp.max(scores, axis=-1, keepdims=True))
    return weights, 1.0 / jnp.sum(weights, axis=-1, keepdims=True)


def sum_kernel(query, keyset, values, cotangent, bias, total):
    own = 2 * bias.shape[1]
    for pair in range(bias.shape[0] // 4):
        tiles = (2 * pair, 2 * pair + 1)
        columns = slice(tiles[0] * own, (tiles[1] + 1) * own)
        wide = jnp.concatenate([bias_tile(bias, tile) for tile in tiles], axis=0)
        summed = None
        for row in range(query.shape[0]):
            weights, inverse = softmax_parts(query[row, :, columns], keyset[row], wide)
            dprobs = lax.dot_general(
                cotangent[row, :, columns], values[row], OUTER, preferred_element_type=jnp.float32
            )
            delta = jnp.sum(weights * dprobs, axis=-1, keepdims=True) * inverse
            dscores = (weights * inverse) * (dprobs - delta)
            summed = dscores if summed is None else summed + dscores
        for index, tile in enumerate(tiles):
            rows = summed[index * own : (index + 1) * own]
            for part, half in enumerate(separate(rolled(rows, FIRST_OUT))):
                total[place(tile, part)] = half.astype(jnp.bfloat16)


def bias_sum(query, keyset, values, cotangent, bias):
    held = pl.BlockSpec(memory_space=pltpu.VMEM)
    return pl.pallas_call(
        sum_kernel,
        in_specs=[held] * 5,
        out_specs=held,
        out_shape=jax.ShapeDtypeStruct(bias.shape, jnp.bfloat16),
        compiler_params=pltpu.CompilerParams(vmem_limit_bytes=LIMIT),
        name="bias_sum",
    )(query, keyset, values, cotangent, bias)


def inputs_kernel(query, keyset, values, cotangent, bias, *refs):
    grad_q, grad_k, grad_v, probs_low, dscores_low = refs
    own = 2 * bias.shape[1]
    scale = DH ** (-0.5)
    for row in range(query.shape[0]):
        for pair in range(bias.shape[0] // 4):
            tiles = (2 * pair, 2 * pair + 1)
            columns = slice(tiles[0] * own, (tiles[1] + 1) * own)
            wide = jnp.concatenate([bias_tile(bias, tile) for tile in tiles], axis=0)
            weights, inverse = softmax_parts(query[row, :, columns], keyset[row], wide)
            probs = weights * inverse
            low = probs.astype(jnp.bfloat16)
            dprobs = lax.dot_general(
                cotangent[row, :, columns], values[row], OUTER, preferred_element_type=jnp.float32
            )
            delta = jnp.sum(low.astype(jnp.float32) * dprobs, axis=-1, keepdims=True)
            probs_low[row, columns] = low
            dscores_low[row, columns] = (probs * (dprobs - delta)).astype(jnp.bfloat16)
    for row in range(query.shape[0]):
        dscores = dscores_low[row]
        turned = lax.dot_general(
            keyset[row], dscores, (((1,), (1,)), ((), ())), preferred_element_type=jnp.float32
        )
        grad_q[row] = (turned * scale).astype(jnp.bfloat16)
        product = jnp.dot(query[row], dscores, preferred_element_type=jnp.float32)
        grad_k[row] = (product * scale).astype(jnp.bfloat16)
        grad_v[row] = jnp.dot(
            cotangent[row], probs_low[row], preferred_element_type=jnp.float32
        ).astype(jnp.bfloat16)


def input_grads(query, keyset, values, cotangent, bias):
    rows, depth, width = query.shape
    held = pl.BlockSpec(memory_space=pltpu.VMEM)
    whole = pl.BlockSpec(query.shape, lambda i: (0, 0, 0))
    shape = jax.ShapeDtypeStruct(query.shape, jnp.bfloat16)
    return pl.pallas_call(
        inputs_kernel,
        grid=(1,),
        in_specs=[held] * 5,
        out_specs=[whole] * 3,
        out_shape=[shape] * 3,
        scratch_shapes=[pltpu.VMEM((rows, width, width), jnp.bfloat16)] * 2,
        compiler_params=pltpu.CompilerParams(vmem_limit_bytes=LIMIT),
        cost_estimate=pl.CostEstimate(
            flops=10 * rows * depth * width * width,
            bytes_accessed=1 << 20,
            transcendentals=rows * width * width,
        ),
        name="input_grads",
    )(query, keyset, values, cotangent, bias)


def fold_kernel(parts, line):
    summed = parts[0].astype(jnp.float32)
    for part in range(1, parts.shape[0]):
        summed = summed + parts[part].astype(jnp.float32)
    rows = line.shape[2]
    for block in range(line.shape[0]):
        low = summed[block * rows : (block + 1) * rows].astype(jnp.bfloat16)
        for copy in range(line.shape[1]):
            line[block, copy] = low


def fold(parts, rows, copies):
    held = pl.BlockSpec(memory_space=pltpu.VMEM)
    shape = (parts.shape[1] // rows, copies, rows, parts.shape[2])
    return pl.pallas_call(
        fold_kernel,
        in_specs=[held],
        out_specs=held,
        out_shape=jax.ShapeDtypeStruct(shape, jnp.bfloat16),
        compiler_params=pltpu.CompilerParams(vmem_limit_bytes=LIMIT),
        name="fold",
    )(parts)


def project_kernel(weight, pair_norm, partial):
    scales = weight[...].astype(jnp.float32)
    wide = pair_norm[...].astype(jnp.float32)
    for head in range(partial.shape[0]):
        partial[head] = jnp.sum(scales[:, head : head + 1][:, :, None] * wide, axis=0)


def project(weight, pair_norm):
    held = pl.BlockSpec(memory_space=pltpu.VMEM)
    return pl.pallas_call(
        project_kernel,
        in_specs=[held, held],
        out_specs=held,
        out_shape=jax.ShapeDtypeStruct(weight.shape[1:] + pair_norm.shape[1:], jnp.float32),
        compiler_params=pltpu.CompilerParams(vmem_limit_bytes=LIMIT),
        name="project",
    )(weight, pair_norm)


def pair_kernel(weight, every_head, grad_pair):
    for head in range(4):
        scale = weight[:, head : head + 1].astype(jnp.float32)[:, :, None]
        term = scale * every_head[head % 2, 1 - head // 2][None]
        if head == 0:
            grad_pair[...] = term
        else:
            grad_pair[...] += term


def pair_grad(weight, every_head):
    held = pl.BlockSpec(memory_space=pltpu.VMEM)
    return pl.pallas_call(
        pair_kernel,
        in_specs=[held, held],
        out_specs=held,
        out_shape=jax.ShapeDtypeStruct(weight.shape[:1] + every_head.shape[2:], jnp.float32),
        compiler_params=pltpu.CompilerParams(vmem_limit_bytes=LIMIT),
        name="pair_grad",
    )(weight, every_head)


def exchange(blocks, axes, order=None):
    groups = None if order is None else [list(order)]
    return lax.all_to_all(blocks, axes, 0, 0, axis_index_groups=groups, tiled=True)


def shards(query, keyset, values, cotangent, pair_norm, bias_weight):
    nz = lax.axis_size("z")
    rows, width = pair_norm.shape[1:]
    query, keyset, values, cotangent = query[0], keyset[0], values[0], cotangent[0]

    partial = jnp.einsum("ch,cjk->hjk", bias_weight, pair_norm, preferred_element_type=jnp.float32)
    own = jnp.sum(exchange(partial, HEAD), axis=0).astype(jnp.bfloat16)
    line = jnp.broadcast_to(own[None], (nz, rows, width))
    line = exchange(line, "z", starting(FIRST_IN, nz)).reshape(nz * rows, width)
    planes = lax.axis_size(PLANE)
    bias = exchange(jnp.broadcast_to(line[None], (planes,) + line.shape), PLANE, PLANE_ORDER)

    total = bias_sum(query, keyset, values, cotangent, bias)
    line = fold(exchange(total, PLANE, PLANE_ORDER), rows, 2)
    order = [2 * z + xl for z in starting(FIRST_OUT, nz) for xl in (1, 0)]
    line = exchange(line.reshape(nz * 2, rows, width), ("z", "xl"), order)
    grads = input_grads(query, keyset, values, cotangent, bias)
    line, *grads = lax.optimization_barrier((line, *grads))
    own = jnp.sum(line.astype(jnp.float32).reshape(nz, 2, rows, width), axis=0)
    every_head = lax.all_gather(own, "core", axis=0)
    grad_pair = pair_grad(bias_weight, every_head)
    return grads[0][None], grads[1][None], grads[2][None], grad_pair


def solution(mesh):
    fine = Mesh(mesh.devices.reshape(4, 16, 2, 2, 2), BLK + HEAD)
    four = P(HEAD, BLK, None, None)
    three = P(HEAD, BLK, None)
    return jax.shard_map(
        shards,
        mesh=fine,
        in_specs=(four, four, four, four, three, P(HEAD, None)),
        out_specs=(four, four, four, three),
        check_vma=False,
    )
```

```python
import math

import jax
import jax.numpy as jnp
from jax import lax
from jax.experimental import pallas as pl
from jax.experimental.pallas import tpu as pltpu
from jax.sharding import Mesh
from jax.sharding import PartitionSpec as P

DH = 32
BLK = ("y", "z", "xh")
HEAD = ("xl", "core")
PLANE = ("y", "xh")
FIRST_IN, FIRST_OUT = 10, 8
PLANE_ORDER = (5, 4, 7, 6, 1, 0, 3, 2)


def starting(first, count):
    return [(first + i) % count for i in range(count)]


def place(y, xh):
    return PLANE_ORDER.index(2 * y + xh)


LIMIT = 24 * 1024 * 1024
LOG2E = math.log2(math.e)
OUTER = (((0,), (0,)), ((), ()))


def first_half(shape):
    return lax.broadcasted_iota(jnp.int32, shape, 1) < shape[1] // 2


def interleave(low, high):
    half = first_half(low.shape)
    even = jnp.where(half, low, pltpu.roll(high, 4, 1))
    odd = jnp.where(half, pltpu.roll(low, 4, 1), high)
    return jnp.stack([even, odd], axis=1).reshape(-1, low.shape[-1])


def separate(rows):
    pairs = rows.reshape(-1, 2, 8, rows.shape[-1])
    even, odd = pairs[:, 0], pairs[:, 1]
    half = first_half(even.shape)
    low = jnp.where(half, even, pltpu.roll(odd, 4, 1))
    high = jnp.where(half, pltpu.roll(even, 4, 1), odd)
    return low.reshape(-1, rows.shape[-1]), high.reshape(-1, rows.shape[-1])


def rolled(rows, blocks):
    cut = 8 * blocks % rows.shape[0]
    return jnp.concatenate([rows[cut:], rows[:cut]], axis=0) if cut else rows


def bias_tile(bias, tile):
    low, high = (
        (bias[place(tile, part)].astype(jnp.float32) * LOG2E).reshape(-1, 8, bias.shape[-1])
        for part in range(2)
    )
    return rolled(interleave(low, high), -FIRST_IN)


def softmax_parts(query, keyset, wide):
    scores = lax.dot_general(query, keyset, OUTER, preferred_element_type=jnp.float32)
    scores = scores * (LOG2E * DH ** (-0.5)) + wide
    weights = jnp.exp2(scores - jnp.max(scores, axis=-1, keepdims=True))
    return weights, 1.0 / jnp.sum(weights, axis=-1, keepdims=True)


def sum_kernel(query, keyset, values, cotangent, bias, total):
    own = 2 * bias.shape[1]
    for pair in range(bias.shape[0] // 4):
        tiles = (2 * pair, 2 * pair + 1)
        columns = slice(tiles[0] * own, (tiles[1] + 1) * own)
        wide = jnp.concatenate([bias_tile(bias, tile) for tile in tiles], axis=0)
        summed = None
        for row in range(query.shape[0]):
            weights, inverse = softmax_parts(query[row, :, columns], keyset[row], wide)
            dprobs = lax.dot_general(
                cotangent[row, :, columns], values[row], OUTER, preferred_element_type=jnp.float32
            )
            delta = jnp.sum(weights * dprobs, axis=-1, keepdims=True) * inverse
            dscores = (weights * inverse) * (dprobs - delta)
            summed = dscores if summed is None else summed + dscores
        for index, tile in enumerate(tiles):
            rows = summed[index * own : (index + 1) * own]
            for part, half in enumerate(separate(rolled(rows, FIRST_OUT))):
                total[place(tile, part)] = half.astype(jnp.bfloat16)


def bias_sum(query, keyset, values, cotangent, bias):
    held = pl.BlockSpec(memory_space=pltpu.VMEM)
    return pl.pallas_call(
        sum_kernel,
        in_specs=[held] * 5,
        out_specs=held,
        out_shape=jax.ShapeDtypeStruct(bias.shape, jnp.bfloat16),
        compiler_params=pltpu.CompilerParams(vmem_limit_bytes=LIMIT),
        name="bias_sum",
    )(query, keyset, values, cotangent, bias)


def inputs_kernel(query, keyset, values, cotangent, bias, *refs):
    grad_q, grad_k, grad_v, probs_low, dscores_low = refs
    own = 2 * bias.shape[1]
    scale = DH ** (-0.5)
    for row in range(query.shape[0]):
        for pair in range(bias.shape[0] // 4):
            tiles = (2 * pair, 2 * pair + 1)
            columns = slice(tiles[0] * own, (tiles[1] + 1) * own)
            wide = jnp.concatenate([bias_tile(bias, tile) for tile in tiles], axis=0)
            weights, inverse = softmax_parts(query[row, :, columns], keyset[row], wide)
            probs = weights * inverse
            low = probs.astype(jnp.bfloat16)
            dprobs = lax.dot_general(
                cotangent[row, :, columns], values[row], OUTER, preferred_element_type=jnp.float32
            )
            delta = jnp.sum(low.astype(jnp.float32) * dprobs, axis=-1, keepdims=True)
            probs_low[row, columns] = low
            dscores_low[row, columns] = (probs * (dprobs - delta)).astype(jnp.bfloat16)
    for row in range(query.shape[0]):
        dscores = dscores_low[row]
        turned = lax.dot_general(
            keyset[row], dscores, (((1,), (1,)), ((), ())), preferred_element_type=jnp.float32
        )
        grad_q[row] = (turned * scale).astype(jnp.bfloat16)
        product = jnp.dot(query[row], dscores, preferred_element_type=jnp.float32)
        grad_k[row] = (product * scale).astype(jnp.bfloat16)
        grad_v[row] = jnp.dot(
            cotangent[row], probs_low[row], preferred_element_type=jnp.float32
        ).astype(jnp.bfloat16)


def input_grads(query, keyset, values, cotangent, bias):
    rows, depth, width = query.shape
    held = pl.BlockSpec(memory_space=pltpu.VMEM)
    whole = pl.BlockSpec(query.shape, lambda i: (0, 0, 0))
    shape = jax.ShapeDtypeStruct(query.shape, jnp.bfloat16)
    return pl.pallas_call(
        inputs_kernel,
        grid=(1,),
        in_specs=[held] * 5,
        out_specs=[whole] * 3,
        out_shape=[shape] * 3,
        scratch_shapes=[pltpu.VMEM((rows, width, width), jnp.bfloat16)] * 2,
        compiler_params=pltpu.CompilerParams(vmem_limit_bytes=LIMIT),
        cost_estimate=pl.CostEstimate(
            flops=10 * rows * depth * width * width,
            bytes_accessed=1 << 20,
            transcendentals=rows * width * width,
        ),
        name="input_grads",
    )(query, keyset, values, cotangent, bias)


def fold_kernel(parts, line):
    summed = parts[0].astype(jnp.float32)
    for part in range(1, parts.shape[0]):
        summed = summed + parts[part].astype(jnp.float32)
    rows = line.shape[2]
    for block in range(line.shape[0]):
        low = summed[block * rows : (block + 1) * rows].astype(jnp.bfloat16)
        for copy in range(line.shape[1]):
            line[block, copy] = low


def fold(parts, rows, copies):
    held = pl.BlockSpec(memory_space=pltpu.VMEM)
    shape = (parts.shape[1] // rows, copies, rows, parts.shape[2])
    return pl.pallas_call(
        fold_kernel,
        in_specs=[held],
        out_specs=held,
        out_shape=jax.ShapeDtypeStruct(shape, jnp.bfloat16),
        compiler_params=pltpu.CompilerParams(vmem_limit_bytes=LIMIT),
        name="fold",
    )(parts)


def project_kernel(weight, pair_norm, partial):
    scales = weight[...].astype(jnp.float32)
    wide = pair_norm[...].astype(jnp.float32)
    for head in range(partial.shape[0]):
        partial[head] = jnp.sum(scales[:, head : head + 1][:, :, None] * wide, axis=0)


def project(weight, pair_norm):
    held = pl.BlockSpec(memory_space=pltpu.VMEM)
    return pl.pallas_call(
        project_kernel,
        in_specs=[held, held],
        out_specs=held,
        out_shape=jax.ShapeDtypeStruct(weight.shape[1:] + pair_norm.shape[1:], jnp.float32),
        compiler_params=pltpu.CompilerParams(vmem_limit_bytes=LIMIT),
        name="project",
    )(weight, pair_norm)


def pair_kernel(weight, every_head, grad_pair):
    for head in range(4):
        scale = weight[:, head : head + 1].astype(jnp.float32)[:, :, None]
        term = scale * every_head[head % 2, 1 - head // 2][None]
        if head == 0:
            grad_pair[...] = term
        else:
            grad_pair[...] += term


def pair_grad(weight, every_head):
    held = pl.BlockSpec(memory_space=pltpu.VMEM)
    return pl.pallas_call(
        pair_kernel,
        in_specs=[held, held],
        out_specs=held,
        out_shape=jax.ShapeDtypeStruct(weight.shape[:1] + every_head.shape[2:], jnp.float32),
        compiler_params=pltpu.CompilerParams(vmem_limit_bytes=LIMIT),
        name="pair_grad",
    )(weight, every_head)


def exchange(blocks, axes, order=None):
    groups = None if order is None else [list(order)]
    return lax.all_to_all(blocks, axes, 0, 0, axis_index_groups=groups, tiled=True)


def shards(query, keyset, values, cotangent, pair_norm, bias_weight):
    nz = lax.axis_size("z")
    rows, width = pair_norm.shape[1:]
    query, keyset, values, cotangent = query[0], keyset[0], values[0], cotangent[0]

    partial = jnp.einsum("ch,cjk->hjk", bias_weight, pair_norm, preferred_element_type=jnp.float32)
    own = jnp.sum(exchange(partial, HEAD), axis=0).astype(jnp.bfloat16)
    line = jnp.broadcast_to(own[None], (nz, rows, width))
    line = exchange(line, "z", starting(FIRST_IN, nz)).reshape(nz * rows, width)
    planes = lax.axis_size(PLANE)
    bias = exchange(jnp.broadcast_to(line[None], (planes,) + line.shape), PLANE, PLANE_ORDER)

    total = bias_sum(query, keyset, values, cotangent, bias)
    line = fold(exchange(total, PLANE, PLANE_ORDER), rows, 2)
    order = [2 * z + xl for z in starting(FIRST_OUT, nz) for xl in (1, 0)]
    line = exchange(line.reshape(nz * 2, rows, width), ("z", "xl"), order)
    grads = input_grads(query, keyset, values, cotangent, bias)
    line, *grads = lax.optimization_barrier((line, *grads))
    own = jnp.sum(line.astype(jnp.float32).reshape(nz, 2, rows, width), axis=0)
    every_head = lax.all_gather(own, "core", axis=0)
    grad_pair = pair_grad(bias_weight, every_head)
    return grads[0][None], grads[1][None], grads[2][None], grad_pair


def solution(mesh):
    fine = Mesh(mesh.devices.reshape(4, 16, 2, 2, 2), BLK + HEAD)
    four = P(HEAD, BLK, None, None)
    three = P(HEAD, BLK, None)
    return jax.shard_map(
        shards,
        mesh=fine,
        in_specs=(four, four, four, four, three, P(HEAD, None)),
        out_specs=(four, four, four, three),
        check_vma=False,
    )
```
